32 devices in a mesh: dom: 2 (over y), ffn: 4 (over z), attn: 4 (over x, core).
Axes of the slice: x: 2, y: 2, z: 4, core: 2. Of those that a mesh axis runs over, the one named last changes fastest.
Arguments:
- queries: bfloat16 [1024, 2048], P(('dom', 'ffn'), 'attn'), parts along dimension 0, may hold values from -6 to 6
- keys: bfloat16 [1024, 2048], P(('dom', 'ffn'), 'attn'), parts along dimension 0, may hold values from -6 to 6
- values: bfloat16 [1024, 2048], P(('dom', 'ffn'), 'attn'), parts along dimension 0, may hold values from -6 to 6
- residual_in: bfloat16 [1024, 2048], P(('dom', 'ffn'), 'attn'), parts along dimension 0, may hold values from -8 to 8
- flow_lengths: int32 [8, 8], P(('dom', 'ffn')), parts along dimension 0, may hold values from 0 to 16, as said below
- out_weight: bfloat16 [2048, 2048], P('attn'), may hold values from -0.125 to 0.125
- gate_weight: bfloat16 [2048, 8192], P(None, 'ffn'), may hold values from -0.125 to 0.125
- up_weight: bfloat16 [2048, 8192], P(None, 'ffn'), may hold values from -0.125 to 0.125
- down_weight: bfloat16 [8192, 2048], P('ffn'), may hold values from -0.0625 to 0.0625
Outputs:
- encoded: bfloat16 [1024, 2048], P(('dom', 'ffn', 'attn')), parts along dimension 0
The draws below stay inside these ranges and needn't reach their ends.
There are 2 independent parts, one for each index of `dom`. The reference program is written for one: setup_inputs(seed, part) draws one part's arguments, and reference() takes and returns one part's arrays. A program takes and returns all parts, laid end to end along the dimension named above; an argument that names none is the same for every part. Nothing has to cross between parts.
Inputs may be any that keep to these rules, and one draw needn't show every extreme that they name: `flow_lengths`: in every group the lengths sum to at most 64, and in some group to exactly 64. The first flow of every group has exactly 16 tokens; a later flow may be empty.
All inputs are finite; a program needn't handle non-finite values.
Results may differ from the reference program's by a relative error of at most 0.015.
Values may be sent and summed in bfloat16 or wider, within the bound.
A program may use at most 128 MiB of HBM per device.

```python
import jax
import jax.numpy as jnp
from jax import lax

D = 2048
FF = 8192
HEAD = 128
TOK_GROUP = 128
FLOWS = 8
LIVE = 64
MOST = 16
TOKENS = 512
N_FFN = 4


def draw_queries(key, part):
    key = jax.random.fold_in(key, 3)
    base = jnp.clip(jax.random.normal(key, (N_FFN, TOK_GROUP, D), jnp.float32), -6.0, 6.0)
    return base.reshape(TOKENS, D).astype(jnp.bfloat16)


def draw_keys(key, part):
    key = jax.random.fold_in(key, 5)
    base = jnp.clip(jax.random.normal(key, (N_FFN, TOK_GROUP, D), jnp.float32), -6.0, 6.0)
    return base.reshape(TOKENS, D).astype(jnp.bfloat16)


def draw_residual_in(key, part):
    key = jax.random.fold_in(key, 7)
    first = jax.random.fold_in(key, 0)
    base = jnp.clip(jax.random.normal(first, (TOKENS, D), jnp.float32), -6.0, 6.0)
    return base.astype(jnp.bfloat16)


def draw_flow_lengths(key, part):
    key = jax.random.fold_in(key, 11)
    first, second, third = jax.random.split(key, 3)
    steps = jax.random.randint(first, (N_FFN, FLOWS), MOST // 2, MOST + 1)
    steps = steps.at[:, 0].set(MOST)
    totals = LIVE - jax.random.randint(second, (N_FFN,), 0, LIVE // 4 + 1)
    full = jax.random.randint(third, (), 0, N_FFN)
    totals = jnp.where(jnp.arange(N_FFN) == full, LIVE, totals)
    ends = jnp.minimum(jnp.cumsum(steps, axis=1), totals[:, None])
    starts = jnp.concatenate([jnp.zeros((N_FFN, 1), jnp.int32), ends[:, :-1]], axis=1)
    return (ends - starts).astype(jnp.int32)


def block_levels(stream_key, dims, pieces, low, largest):
    def one(axis_at, blocks):
        steps = jax.random.uniform(jax.random.fold_in(jax.random.fold_in(stream_key, 6), axis_at), (blocks,), jnp.float32, low / len(pieces), largest / len(pieces))
        return jnp.repeat(jnp.exp(steps), dims[axis_at] // blocks).reshape((-1,) + (1,) * (len(dims) - axis_at - 1))

    gain = one(*pieces[0])
    for cut in pieces[1:]:
        gain = gain * one(*cut)
    return gain


def bell_draw(rng, dims, scale, bound, cuts=(), kind=jnp.bfloat16):
    values = scale * jax.random.normal(rng, dims, jnp.float32)
    if cuts:
        values = values * block_levels(rng, dims, cuts, -0.22, 0.18)
    return jnp.clip(values, -bound, bound).astype(kind)


def setup_inputs(seed: int = 0, part: int = 0) -> dict:
    streams_of = jax.random.split(jax.random.key(seed), 10)
    part_splits = jax.random.split(jax.random.fold_in(streams_of[9], part), 10)
    queries = draw_queries(jax.random.fold_in(jax.random.fold_in(streams_of[9], part), 71), part)
    keys = draw_keys(jax.random.fold_in(jax.random.fold_in(streams_of[9], part), 71), part)
    values = bell_draw(part_splits[2], (TOKENS, D), 1.0, 6.0, ((0, 4), (1, 4)))
    residual_in = draw_residual_in(jax.random.fold_in(jax.random.fold_in(streams_of[9], part), 71), part)
    flow_lengths = draw_flow_lengths(jax.random.fold_in(jax.random.fold_in(streams_of[9], part), 71), part)
    out_weight = bell_draw(streams_of[5], (D, D), D ** -0.5, 0.125, ((0, 4),))
    gate_weight = bell_draw(streams_of[6], (D, FF), D ** -0.5, 0.125, ((1, 4),))
    up_weight = bell_draw(streams_of[7], (D, FF), D ** -0.5, 0.125, ((1, 4),))
    down_weight = bell_draw(streams_of[8], (FF, D), FF ** -0.5, 0.0625, ((0, 4),))
    return {"queries": queries, "keys": keys, "values": values, "residual_in": residual_in, "flow_lengths": flow_lengths, "out_weight": out_weight, "gate_weight": gate_weight, "up_weight": up_weight, "down_weight": down_weight}


def flow_segments(lengths, count):
    ends = jnp.cumsum(lengths)
    positions = jnp.arange(count, dtype=jnp.int32)
    segment = lax.optimization_barrier(jnp.sum((ends[None, :] <= positions[:, None]).astype(jnp.int32), axis=1))
    return (segment, positions < ends[-1])

def attend(query_rows, key_rows, value_rows, segment):
    count = query_rows.shape[0]
    heads = query_rows.shape[1] // HEAD
    query_f = query_rows.astype(jnp.float32).reshape(count, heads, HEAD)
    key_f = key_rows.astype(jnp.float32).reshape(count, heads, HEAD)
    value_f = value_rows.astype(jnp.float32).reshape(count, heads, HEAD)
    scores = jnp.einsum('qhd,khd->hqk', query_f, key_f) * HEAD ** (-0.5)
    same = segment[:, None] == segment[None, :]
    scores = jnp.where(same[None], scores, -jnp.inf)
    top = lax.optimization_barrier(jnp.max(scores, axis=2, keepdims=True))
    weights = jnp.exp(scores - top)
    weights = weights / lax.optimization_barrier(jnp.sum(weights, axis=2, keepdims=True))
    probs = lax.optimization_barrier(weights.astype(jnp.bfloat16)).astype(jnp.float32)
    mixed = jnp.einsum('hqk,khd->qhd', probs, value_f)
    return mixed.reshape(count, heads * HEAD).astype(jnp.bfloat16)

def reference(queries, keys, values, residual_in, flow_lengths, out_weight, gate_weight, up_weight, down_weight):
    groups = flow_lengths.shape[0]
    group_rows = queries.shape[0] // groups

    def one_group(index):
        start = (index * group_rows).astype(jnp.int32)
        query_rows = lax.dynamic_slice_in_dim(queries, start, group_rows, 0)
        key_rows = lax.dynamic_slice_in_dim(keys, start, group_rows, 0)
        value_rows = lax.dynamic_slice_in_dim(values, start, group_rows, 0)
        segment, live = flow_segments(flow_lengths[index], group_rows)
        return (attend(query_rows, key_rows, value_rows, segment), live)
    mixed, live = lax.map(one_group, jnp.arange(groups, dtype=jnp.int32))
    mixed = mixed.reshape(queries.shape[0], queries.shape[1])
    live = live.reshape(queries.shape[0])
    state = residual_in.astype(jnp.float32) + jnp.dot(mixed, out_weight, preferred_element_type=jnp.float32)
    scale = lax.rsqrt(lax.optimization_barrier(jnp.mean(state * state, axis=1, keepdims=True)) + 1e-06)
    normed = (state * scale).astype(jnp.bfloat16)
    gate = jnp.dot(normed, gate_weight, preferred_element_type=jnp.float32)
    up_part = jnp.dot(normed, up_weight, preferred_element_type=jnp.float32)
    hidden = (jax.nn.silu(gate) * up_part).astype(jnp.bfloat16)
    block = FF // N_FFN

    def add_block(total, index):
        start = (index * block).astype(jnp.int32)
        hidden_block = lax.dynamic_slice_in_dim(hidden, start, block, 1)
        down_block = lax.dynamic_slice_in_dim(down_weight, start, block, 0)
        term = jnp.dot(hidden_block, down_block, preferred_element_type=jnp.float32)
        term = lax.optimization_barrier(term.astype(jnp.bfloat16)).astype(jnp.float32)
        return (total + term, None)
    feed, unused = lax.scan(add_block, jnp.zeros(state.shape, jnp.float32), jnp.arange(N_FFN, dtype=jnp.int32))
    return jnp.where(live[:, None], state + feed, 0.0).astype(jnp.bfloat16)
```

```python
import functools

import jax
import jax.numpy as jnp
from jax import lax
from jax.experimental import pallas as pl
from jax.experimental.pallas import tpu as pltpu
from jax.sharding import PartitionSpec as P

HEAD = 128
LIVE = 64
ROWS = 16
PARTS = LIVE // ROWS
MESH = pl.DeviceIdType.MESH
F32 = jnp.float32
BF16 = jnp.bfloat16


def widths(total, width):
    width = min(width, total)
    return [(at, width) for at in range(0, total, width)]


def layer(
    n_attn,
    n_ffn,
    q_hbm,
    k_hbm,
    v_hbm,
    res_hbm,
    lens,
    wo_hbm,
    wg_hbm,
    wu_hbm,
    wd_hbm,
    out,
    q,
    k,
    v,
    res,
    wo,
    wg,
    wu,
    wd,
    mixed,
    term,
    term16,
    got1,
    state,
    rows,
    gate,
    up,
    hidden,
    part16,
    got2,
    done16,
    in_sem,
    gate_sem,
    up_sem,
    down_sem,
    send1,
    recv1,
    send2,
    recv2,
    send3,
    recv3,
    send4,
    recv4,
):
    a = lax.axis_index("attn")
    z = lax.axis_index("ffn")
    width = q.shape[1]
    model = wo.shape[1]
    units = wg.shape[1]
    share = out.shape[0]
    part = lax.rem(a, PARTS)
    own_rows = pl.ds(pl.multiple_of(part * ROWS, ROWS), ROWS)

    barrier = pltpu.get_barrier_semaphore()
    for step in range(1, n_attn):
        pl.semaphore_signal(
            barrier, inc=1, device_id={"attn": lax.rem(a + step, n_attn)}, device_id_type=MESH
        )
    for step in range(1, n_ffn):
        pl.semaphore_signal(
            barrier, inc=1, device_id={"ffn": lax.rem(z + step, n_ffn)}, device_id_type=MESH
        )

    live_rows = pl.ds(0, LIVE)
    small = [
        pltpu.make_async_copy(src.at[live_rows, :], dst, in_sem.at[i])
        for i, (src, dst) in enumerate(((q_hbm, q), (k_hbm, k), (v_hbm, v), (res_hbm, res)))
    ]
    small.append(pltpu.make_async_copy(wo_hbm, wo, in_sem.at[4]))
    for copy in small:
        copy.start()
    deep = widths(model, 512)
    wide = widths(model, 512)
    gate_in = [
        pltpu.make_async_copy(wg_hbm.at[pl.ds(at, w), :], wg.at[pl.ds(at, w), :], gate_sem.at[i])
        for i, (at, w) in enumerate(deep)
    ]
    up_in = [
        pltpu.make_async_copy(wu_hbm.at[pl.ds(at, w), :], wu.at[pl.ds(at, w), :], up_sem.at[i])
        for i, (at, w) in enumerate(deep)
    ]
    down_in = [
        pltpu.make_async_copy(wd_hbm.at[:, pl.ds(at, w)], wd.at[:, pl.ds(at, w)], down_sem.at[i])
        for i, (at, w) in enumerate(wide)
    ]
    for copy in small[:3]:
        copy.wait()
    for one, two in zip(gate_in, up_in):
        one.start()
        two.start()
    for copy in down_in:
        copy.start()

    row_at = lax.broadcasted_iota(jnp.int32, (LIVE, LIVE), 0)
    col_at = lax.broadcasted_iota(jnp.int32, (LIVE, LIVE), 1)
    row_flow = jnp.zeros((LIVE, LIVE), jnp.int32)
    col_flow = jnp.zeros((LIVE, LIVE), jnp.int32)
    end = jnp.int32(0)
    for flow in range(lens.shape[1]):
        end = end + lens[0, flow]
        row_flow += (row_at >= end).astype(jnp.int32)
        col_flow += (col_at >= end).astype(jnp.int32)
    total_live = end
    same = row_flow == col_flow
    for head in range(width // HEAD):
        cols = slice(head * HEAD, (head + 1) * HEAD)
        scores = lax.dot_general(
            q[:, cols], k[:, cols], (((1,), (1,)), ((), ())), preferred_element_type=F32
        ) * HEAD ** (-0.5)
        scores = jnp.where(same, scores, -jnp.inf)
        weights = jnp.exp(scores - jnp.max(scores, axis=1, keepdims=True))
        probs = (weights / jnp.sum(weights, axis=1, keepdims=True)).astype(BF16)
        mixed[:, cols] = jnp.dot(probs, v[:, cols], preferred_element_type=F32).astype(BF16)

    small[3].wait()
    small[4].wait()
    pl.semaphore_wait(barrier, n_attn + n_ffn - 2)
    sent = []
    first = []
    for i, (at, w) in enumerate(wide):
        for sub in range(at, at + w, width):
            cols = slice(sub, sub + width)
            value = jnp.dot(mixed[...], wo[:, cols], preferred_element_type=F32)
            value += jnp.where(a == sub // width, res[...].astype(F32), 0.0)
            term[:, cols] = value
            term16[:, cols] = value.astype(BF16)
        for step in range(1, n_attn):
            peer = lax.rem(a + step, n_attn)
            peer_rows = pl.ds(pl.multiple_of(lax.rem(peer, PARTS) * ROWS, ROWS), ROWS)
            copy = pltpu.make_async_remote_copy(
                src_ref=term16.at[peer_rows, pl.ds(at, w)],
                dst_ref=got1.at[step - 1, :, pl.ds(at, w)],
                send_sem=send1.at[step - 1, i],
                recv_sem=recv1.at[step - 1, i],
                device_id={"attn": peer},
                device_id_type=MESH,
            )
            copy.start()
            sent.append(copy)
            first.append(copy)
    squares = jnp.zeros((ROWS, 1), F32)
    for i, (at, w) in enumerate(wide):
        cols = slice(at, at + w)
        value = term[own_rows, cols]
        for step in range(1, n_attn):
            first[i * (n_attn - 1) + step - 1].wait_recv()
            value += got1[step - 1, :, cols].astype(F32)
        state[:, cols] = value
        squares += jnp.sum(value * value, axis=1, keepdims=True)
    scale = lax.rsqrt(squares / model + 1e-06)

    second = []
    for i, (at, w) in enumerate(deep):
        rows[0:ROWS, at : at + w] = (state[:, at : at + w] * scale).astype(BF16)
        for step in range(1, n_ffn):
            copy = pltpu.make_async_remote_copy(
                src_ref=rows.at[pl.ds(0, ROWS), pl.ds(at, w)],
                dst_ref=rows.at[pl.ds(step * ROWS, ROWS), pl.ds(at, w)],
                send_sem=send2.at[step - 1, i],
                recv_sem=recv2.at[step - 1, i],
                device_id={"ffn": lax.rem(z + step, n_ffn)},
                device_id_type=MESH,
            )
            copy.start()
            sent.append(copy)
            second.append(copy)

    for i, (at, w) in enumerate(deep):
        gate_in[i].wait()
        up_in[i].wait()
        for step in range(1, n_ffn):
            second[i * (n_ffn - 1) + step - 1].wait_recv()
        for col, cw in widths(units, 512):
            cols = slice(col, col + cw)
            piece = rows[:, at : at + w]
            g = jnp.dot(piece, wg[at : at + w, cols], preferred_element_type=F32)
            u = jnp.dot(piece, wu[at : at + w, cols], preferred_element_type=F32)
            if i > 0:
                g += gate[:, cols]
                u += up[:, cols]
            if i < len(deep) - 1:
                gate[:, cols] = g
                up[:, cols] = u
            else:
                hidden[:, cols] = (g / (1.0 + jnp.exp(-g)) * u).astype(BF16)

    third = []
    for i, (at, w) in enumerate(wide):
        cols = slice(at, at + w)
        down_in[i].wait()
        part16[:, cols] = jnp.dot(hidden[...], wd[:, cols], preferred_element_type=F32).astype(BF16)
        for step in range(1, n_ffn):
            copy = pltpu.make_async_remote_copy(
                src_ref=part16.at[pl.ds(step * ROWS, ROWS), pl.ds(at, w)],
                dst_ref=got2.at[step - 1, :, pl.ds(at, w)],
                send_sem=send3.at[step - 1, i],
                recv_sem=recv3.at[step - 1, i],
                device_id={"ffn": lax.rem(z + n_ffn - step, n_ffn)},
                device_id_type=MESH,
            )
            copy.start()
            sent.append(copy)
            third.append(copy)

    @pl.when(a * share >= LIVE)
    def _():
        out[...] = jnp.zeros_like(out)

    live = part * ROWS + lax.broadcasted_iota(jnp.int32, (ROWS, 1), 0) < total_live

    def last(p, i, at, w):
        return pltpu.make_async_remote_copy(
            src_ref=done16.at[:, pl.ds(at, w)],
            dst_ref=out.at[pl.ds(p * ROWS % share, ROWS), pl.ds(at, w)],
            send_sem=send4.at[i],
            recv_sem=recv4.at[p, i],
            device_id={"attn": p * ROWS // share},
            device_id_type=MESH,
        )

    for i, (at, w) in enumerate(wide):
        cols = slice(at, at + w)
        feed = part16[0:ROWS, cols].astype(F32)
        for step in range(1, n_ffn):
            third[i * (n_ffn - 1) + step - 1].wait_recv()
            feed += got2[step - 1, :, cols].astype(F32)
        done16[:, cols] = jnp.where(live, state[:, cols] + feed, 0.0).astype(BF16)
        for p in range(PARTS):
            owner = p * ROWS // share

            @pl.when(a == p)
            def _():
                if owner == p:
                    out[p * ROWS % share : p * ROWS % share + ROWS, cols] = done16[:, cols]
                else:
                    last(p, i, at, w).start()

    for copy in sent:
        copy.wait_send()
    for p in range(PARTS):
        owner = p * ROWS // share
        if owner != p:

            @pl.when(a == p)
            def _():
                for i, (at, w) in enumerate(wide):
                    last(p, i, at, w).wait_send()

            @pl.when(a == owner)
            def _():
                for i, (at, w) in enumerate(wide):
                    last(p, i, at, w).wait_recv()


def on_device(n_attn, n_ffn, q, k, v, res, lens, wo, wg, wu, wd):
    group, width = q.shape
    model = wo.shape[1]
    units = wg.shape[1]
    share = group // n_attn
    tokens = n_ffn * ROWS
    pieces = max(1, model // 512)
    any_space = pl.BlockSpec(memory_space=pl.ANY)
    dma = pltpu.SemaphoreType.DMA
    return pl.pallas_call(
        functools.partial(layer, n_attn, n_ffn),
        out_shape=jax.ShapeDtypeStruct((share, model), BF16),
        in_specs=[any_space] * 4 + [pl.BlockSpec(memory_space=pltpu.SMEM)] + [any_space] * 4,
        out_specs=pl.BlockSpec(memory_space=pltpu.VMEM),
        scratch_shapes=[
            pltpu.VMEM((LIVE, width), BF16),
            pltpu.VMEM((LIVE, width), BF16),
            pltpu.VMEM((LIVE, width), BF16),
            pltpu.VMEM((LIVE, width), BF16),
            pltpu.VMEM((width, model), BF16),
            pltpu.VMEM((model, units), BF16),
            pltpu.VMEM((model, units), BF16),
            pltpu.VMEM((units, model), BF16),
            pltpu.VMEM((LIVE, width), BF16),
            pltpu.VMEM((LIVE, model), F32),
            pltpu.VMEM((LIVE, model), BF16),
            pltpu.VMEM((n_attn - 1, ROWS, model), BF16),
            pltpu.VMEM((ROWS, model), F32),
            pltpu.VMEM((tokens, model), BF16),
            pltpu.VMEM((tokens, units), F32),
            pltpu.VMEM((tokens, units), F32),
            pltpu.VMEM((tokens, units), BF16),
            pltpu.VMEM((tokens, model), BF16),
            pltpu.VMEM((n_ffn - 1, ROWS, model), BF16),
            pltpu.VMEM((ROWS, model), BF16),
            dma((5,)),
            dma((pieces,)),
            dma((pieces,)),
            dma((pieces,)),
            dma((n_attn - 1, pieces)),
            dma((n_attn - 1, pieces)),
            dma((n_ffn - 1, pieces)),
            dma((n_ffn - 1, pieces)),
            dma((n_ffn - 1, pieces)),
            dma((n_ffn - 1, pieces)),
            dma((pieces,)),
            dma((PARTS, pieces)),
        ],
        compiler_params=pltpu.CompilerParams(
            collective_id=0, has_side_effects=True, vmem_limit_bytes=56 * 1024 * 1024
        ),
        cost_estimate=pl.CostEstimate(
            flops=2 * tokens * 3 * model * units + 2 * LIVE * width * model,
            bytes_accessed=2 * (3 * model * units + width * model),
            transcendentals=tokens * units,
        ),
    )(q, k, v, res, lens, wo, wg, wu, wd)


def solution(mesh):
    rows_split = P(("dom", "ffn"), "attn")
    placed = (
        rows_split,
        rows_split,
        rows_split,
        rows_split,
        P(("dom", "ffn"), None),
        P("attn", None),
        P(None, "ffn"),
        P(None, "ffn"),
        P("ffn", None),
    )
    return jax.shard_map(
        functools.partial(on_device, mesh.shape["attn"], mesh.shape["ffn"]),
        mesh=mesh,
        in_specs=placed,
        out_specs=P(("dom", "ffn", "attn"), None),
        check_vma=False,
    )
```

```python
import functools

import jax
import jax.numpy as jnp
from jax import lax
from jax.experimental import pallas as pl
from jax.experimental.pallas import tpu as pltpu
from jax.sharding import PartitionSpec as P

HEAD = 128
LIVE = 64
ROWS = 16
PARTS = LIVE // ROWS
MESH = pl.DeviceIdType.MESH
F32 = jnp.float32
BF16 = jnp.bfloat16


def widths(total, width):
    width = min(width, total)
    return [(at, width) for at in range(0, total, width)]


def layer(
    n_attn,
    n_ffn,
    q_hbm,
    k_hbm,
    v_hbm,
    res_hbm,
    lens,
    wo_hbm,
    wg_hbm,
    wu_hbm,
    wd_hbm,
    out,
    q,
    k,
    v,
    res,
    wo,
    wg,
    wu,
    wd,
    mixed,
    term,
    term16,
    got1,
    state,
    rows,
    gate,
    up,
    hidden,
    part16,
    got2,
    held,
    in_sem,
    gate_sem,
    up_sem,
    down_sem,
    send1,
    recv1,
    send2,
    recv2,
    send3,
    recv3,
    send4,
    recv4,
):
    a = lax.axis_index("attn")
    z = lax.axis_index("ffn")
    width = q.shape[1]
    model = wo.shape[1]
    units = wg.shape[1]
    share = out.shape[0]
    part = lax.rem(a, PARTS)
    owner = part * ROWS // share
    place = lax.rem(part * ROWS, share) // ROWS
    away = jnp.logical_and(a < PARTS, a != owner)
    own_rows = pl.ds(pl.multiple_of(part * ROWS, ROWS), ROWS)

    barrier = pltpu.get_barrier_semaphore()
    for far in range(n_ffn):
        for step in range(n_attn):
            if far or step:
                peer = {"ffn": lax.rem(z + far, n_ffn), "attn": lax.rem(a + step, n_attn)}
                pl.semaphore_signal(barrier, inc=1, device_id=peer, device_id_type=MESH)

    live_rows = pl.ds(0, LIVE)
    small = [
        pltpu.make_async_copy(src.at[live_rows, :], dst, in_sem.at[i])
        for i, (src, dst) in enumerate(((q_hbm, q), (k_hbm, k), (v_hbm, v), (res_hbm, res)))
    ]
    small.append(pltpu.make_async_copy(wo_hbm, wo, in_sem.at[4]))
    for copy in small:
        copy.start()
    deep = widths(model, 512)
    wide = widths(model, 512)
    gate_in = [
        pltpu.make_async_copy(wg_hbm.at[pl.ds(at, w), :], wg.at[pl.ds(at, w), :], gate_sem.at[i])
        for i, (at, w) in enumerate(deep)
    ]
    up_in = [
        pltpu.make_async_copy(wu_hbm.at[pl.ds(at, w), :], wu.at[pl.ds(at, w), :], up_sem.at[i])
        for i, (at, w) in enumerate(deep)
    ]
    down_in = [
        pltpu.make_async_copy(wd_hbm.at[:, pl.ds(at, w)], wd.at[:, pl.ds(at, w)], down_sem.at[i])
        for i, (at, w) in enumerate(wide)
    ]
    for copy in small[:3]:
        copy.wait()
    for one, two in zip(gate_in, up_in):
        one.start()
        two.start()
    for copy in down_in:
        copy.start()

    row_at = lax.broadcasted_iota(jnp.int32, (LIVE, LIVE), 0)
    col_at = lax.broadcasted_iota(jnp.int32, (LIVE, LIVE), 1)
    row_flow = jnp.zeros((LIVE, LIVE), jnp.int32)
    col_flow = jnp.zeros((LIVE, LIVE), jnp.int32)
    end = jnp.int32(0)
    for flow in range(lens.shape[1]):
        end = end + lens[0, flow]
        row_flow += (row_at >= end).astype(jnp.int32)
        col_flow += (col_at >= end).astype(jnp.int32)
    total_live = end
    same = row_flow == col_flow
    for head in range(width // HEAD):
        cols = slice(head * HEAD, (head + 1) * HEAD)
        scores = lax.dot_general(
            q[:, cols], k[:, cols], (((1,), (1,)), ((), ())), preferred_element_type=F32
        ) * HEAD ** (-0.5)
        scores = jnp.where(same, scores, -jnp.inf)
        weights = jnp.exp(scores - jnp.max(scores, axis=1, keepdims=True))
        probs = (weights / jnp.sum(weights, axis=1, keepdims=True)).astype(BF16)
        mixed[:, cols] = jnp.dot(probs, v[:, cols], preferred_element_type=F32).astype(BF16)

    small[3].wait()
    small[4].wait()
    pl.semaphore_wait(barrier, n_attn * n_ffn - 1)
    sent = []
    first = []
    for i, (at, w) in enumerate(wide):
        for sub in range(at, at + w, width):
            cols = slice(sub, sub + width)
            value = jnp.dot(mixed[...], wo[:, cols], preferred_element_type=F32)
            value += jnp.where(a == sub // width, res[...].astype(F32), 0.0)
            term[:, cols] = value
            term16[:, cols] = value.astype(BF16)
        for step in range(1, n_attn):
            peer = lax.rem(a + step, n_attn)
            peer_rows = pl.ds(pl.multiple_of(lax.rem(peer, PARTS) * ROWS, ROWS), ROWS)
            copy = pltpu.make_async_remote_copy(
                src_ref=term16.at[peer_rows, pl.ds(at, w)],
                dst_ref=got1.at[step - 1, :, pl.ds(at, w)],
                send_sem=send1.at[step - 1, i],
                recv_sem=recv1.at[step - 1, i],
                device_id={"attn": peer},
                device_id_type=MESH,
            )
            copy.start()
            sent.append(copy)
            first.append(copy)

    second = []
    for i, (at, w) in enumerate(deep):
        cols = slice(at, at + w)
        value = term[own_rows, cols]
        for step in range(1, n_attn):
            first[i * (n_attn - 1) + step - 1].wait_recv()
            value += got1[step - 1, :, cols].astype(F32)
        state[:, cols] = value
        rows[0:ROWS, cols] = value.astype(BF16)
        for step in range(1, n_ffn):
            copy = pltpu.make_async_remote_copy(
                src_ref=rows.at[pl.ds(0, ROWS), pl.ds(at, w)],
                dst_ref=rows.at[pl.ds(step * ROWS, ROWS), pl.ds(at, w)],
                send_sem=send2.at[step - 1, i],
                recv_sem=recv2.at[step - 1, i],
                device_id={"ffn": lax.rem(z + step, n_ffn)},
                device_id_type=MESH,
            )
            copy.start()
            sent.append(copy)
            second.append(copy)
    state_copy = pltpu.make_async_remote_copy(
        src_ref=state,
        dst_ref=held.at[place],
        send_sem=send4.at[0],
        recv_sem=recv4.at[place],
        device_id={"attn": owner},
        device_id_type=MESH,
    )

    @pl.when(away)
    def _():
        state_copy.start()

    @pl.when(a == owner)
    def _():
        held[place] = state[...]

    squares = jnp.zeros((n_ffn * ROWS, 1), F32)
    for i, (at, w) in enumerate(deep):
        gate_in[i].wait()
        up_in[i].wait()
        for step in range(1, n_ffn):
            second[i * (n_ffn - 1) + step - 1].wait_recv()
        piece = rows[:, at : at + w]
        squares += jnp.sum(piece.astype(F32) * piece.astype(F32), axis=1, keepdims=True)
        scale = lax.rsqrt(squares / model + 1e-06)
        for col, cw in widths(units, 512):
            cols = slice(col, col + cw)
            g = jnp.dot(piece, wg[at : at + w, cols], preferred_element_type=F32)
            u = jnp.dot(piece, wu[at : at + w, cols], preferred_element_type=F32)
            if i > 0:
                g += gate[:, cols]
                u += up[:, cols]
            if i < len(deep) - 1:
                gate[:, cols] = g
                up[:, cols] = u
            else:
                g *= scale
                u *= scale
                hidden[:, cols] = (g / (1.0 + jnp.exp(-g)) * u).astype(BF16)

    def partial(step, i, at, w):
        return pltpu.make_async_remote_copy(
            src_ref=part16.at[pl.ds(step * ROWS, ROWS), pl.ds(at, w)],
            dst_ref=got2.at[place, step, :, pl.ds(at, w)],
            send_sem=send3.at[step, i],
            recv_sem=recv3.at[place, step, i],
            device_id={"ffn": lax.rem(z + n_ffn - step, n_ffn), "attn": owner},
            device_id_type=MESH,
        )

    for i, (at, w) in enumerate(wide):
        cols = slice(at, at + w)
        down_in[i].wait()
        part16[:, cols] = jnp.dot(hidden[...], wd[:, cols], preferred_element_type=F32).astype(BF16)

        @pl.when(a < PARTS)
        def _():
            for step in range(1, n_ffn):
                partial(step, i, at, w).start()

        @pl.when(away)
        def _():
            partial(0, i, at, w).start()

        @pl.when(a == owner)
        def _():
            got2[place, 0, :, cols] = part16[0:ROWS, cols]

    per = share // ROWS

    @pl.when(a * share >= LIVE)
    def _():
        out[...] = jnp.zeros_like(out)

    @pl.when(a * share < LIVE)
    def _():
        def arrival(q, step, i, at, w):
            return pltpu.make_async_remote_copy(
                src_ref=part16.at[pl.ds(step * ROWS, ROWS), pl.ds(at, w)],
                dst_ref=got2.at[q, step, :, pl.ds(at, w)],
                send_sem=send3.at[step, i],
                recv_sem=recv3.at[q, step, i],
                device_id={"attn": owner},
                device_id_type=MESH,
            )

        for q in range(per):

            @pl.when(a * per + q != a)
            def _():
                pltpu.make_async_remote_copy(
                    src_ref=state,
                    dst_ref=held.at[q],
                    send_sem=send4.at[0],
                    recv_sem=recv4.at[q],
                    device_id={"attn": owner},
                    device_id_type=MESH,
                ).wait_recv()

        at_row = lax.broadcasted_iota(jnp.int32, (ROWS, 1), 0)
        for i, (at, w) in enumerate(wide):
            cols = slice(at, at + w)
            for q in range(per):

                @pl.when(a * per + q != a)
                def _():
                    arrival(q, 0, i, at, w).wait_recv()

                for step in range(1, n_ffn):
                    arrival(q, step, i, at, w).wait_recv()
                feed = got2[q, 0, :, cols].astype(F32)
                for step in range(1, n_ffn):
                    feed += got2[q, step, :, cols].astype(F32)
                live = (a * per + q) * ROWS + at_row < total_live
                value = jnp.where(live, held[q, :, cols] + feed, 0.0)
                out[q * ROWS : (q + 1) * ROWS, cols] = value.astype(BF16)

    for copy in sent:
        copy.wait_send()

    @pl.when(a < PARTS)
    def _():
        for i, (at, w) in enumerate(wide):
            for step in range(1, n_ffn):
                partial(step, i, at, w).wait_send()

    @pl.when(away)
    def _():
        state_copy.wait_send()
        for i, (at, w) in enumerate(wide):
            partial(0, i, at, w).wait_send()


def on_device(n_attn, n_ffn, q, k, v, res, lens, wo, wg, wu, wd):
    group, width = q.shape
    model = wo.shape[1]
    units = wg.shape[1]
    share = group // n_attn
    tokens = n_ffn * ROWS
    per = share // ROWS
    pieces = max(1, model // 512)
    any_space = pl.BlockSpec(memory_space=pl.ANY)
    dma = pltpu.SemaphoreType.DMA
    return pl.pallas_call(
        functools.partial(layer, n_attn, n_ffn),
        out_shape=pltpu.VMEM((share, model), BF16),
        in_specs=[any_space] * 4 + [pl.BlockSpec(memory_space=pltpu.SMEM)] + [any_space] * 4,
        out_specs=pl.BlockSpec(memory_space=pltpu.VMEM),
        scratch_shapes=[
            pltpu.VMEM((LIVE, width), BF16),
            pltpu.VMEM((LIVE, width), BF16),
            pltpu.VMEM((LIVE, width), BF16),
            pltpu.VMEM((LIVE, width), BF16),
            pltpu.VMEM((width, model), BF16),
            pltpu.VMEM((model, units), BF16),
            pltpu.VMEM((model, units), BF16),
            pltpu.VMEM((units, model), BF16),
            pltpu.VMEM((LIVE, width), BF16),
            pltpu.VMEM((LIVE, model), F32),
            pltpu.VMEM((LIVE, model), BF16),
            pltpu.VMEM((n_attn - 1, ROWS, model), BF16),
            pltpu.VMEM((ROWS, model), F32),
            pltpu.VMEM((tokens, model), BF16),
            pltpu.VMEM((tokens, units), F32),
            pltpu.VMEM((tokens, units), F32),
            pltpu.VMEM((tokens, units), BF16),
            pltpu.VMEM((tokens, model), BF16),
            pltpu.VMEM((per, n_ffn, ROWS, model), BF16),
            pltpu.VMEM((per, ROWS, model), F32),
            dma((5,)),
            dma((pieces,)),
            dma((pieces,)),
            dma((pieces,)),
            dma((n_attn - 1, pieces)),
            dma((n_attn - 1, pieces)),
            dma((n_ffn - 1, pieces)),
            dma((n_ffn - 1, pieces)),
            dma((n_ffn, pieces)),
            dma((per, n_ffn, pieces)),
            dma((1,)),
            dma((per,)),
        ],
        compiler_params=pltpu.CompilerParams(
            collective_id=0, has_side_effects=True, vmem_limit_bytes=56 * 1024 * 1024
        ),
        cost_estimate=pl.CostEstimate(
            flops=2 * tokens * 3 * model * units + 2 * LIVE * width * model,
            bytes_accessed=2 * (3 * model * units + width * model),
            transcendentals=tokens * units,
        ),
    )(q, k, v, res, lens, wo, wg, wu, wd)


def solution(mesh):
    rows_split = P(("dom", "ffn"), "attn")
    placed = (
        rows_split,
        rows_split,
        rows_split,
        rows_split,
        P(("dom", "ffn"), None),
        P("attn", None),
        P(None, "ffn"),
        P(None, "ffn"),
        P("ffn", None),
    )
    return jax.shard_map(
        functools.partial(on_device, mesh.shape["attn"], mesh.shape["ffn"]),
        mesh=mesh,
        in_specs=placed,
        out_specs=P(("dom", "ffn", "attn"), None),
        check_vma=False,
    )
```

```python
import functools

import jax
import jax.numpy as jnp
from jax import lax
from jax.experimental import pallas as pl
from jax.experimental.pallas import tpu as pltpu
from jax.sharding import PartitionSpec as P

HEAD = 128
LIVE = 64
ROWS = 16
PARTS = LIVE // ROWS
MESH = pl.DeviceIdType.MESH
F32 = jnp.float32
BF16 = jnp.bfloat16


def widths(total, width):
    width = min(width, total)
    return [(at, width) for at in range(0, total, width)]


def layer(
    n_attn,
    n_ffn,
    q_hbm,
    k_hbm,
    v_hbm,
    res_hbm,
    lens,
    wo_hbm,
    wg_hbm,
    wu_hbm,
    wd_hbm,
    out,
    q,
    k,
    v,
    res,
    wo,
    wg,
    wu,
    wd,
    mixed,
    term,
    term16,
    got1,
    state,
    rows,
    gate,
    up,
    hidden,
    part16,
    got2,
    held,
    in_sem,
    gate_sem,
    up_sem,
    down_sem,
    send1,
    recv1,
    send2,
    recv2,
    send3,
    recv3,
    send4,
    recv4,
):
    a = lax.axis_index("attn")
    z = lax.axis_index("ffn")
    width = q.shape[1]
    model = wo.shape[1]
    units = wg.shape[1]
    share = out.shape[0]
    part = lax.rem(a, PARTS)
    owner = part * ROWS // share
    place = lax.rem(part * ROWS, share) // ROWS
    away = jnp.logical_and(a < PARTS, a != owner)
    own_rows = pl.ds(pl.multiple_of(part * ROWS, ROWS), ROWS)

    barrier = pltpu.get_barrier_semaphore()
    for far in range(n_ffn):
        for step in range(n_attn):
            if far or step:
                peer = {"ffn": lax.rem(z + far, n_ffn), "attn": lax.rem(a + step, n_attn)}
                pl.semaphore_signal(barrier, inc=1, device_id=peer, device_id_type=MESH)

    live_rows = pl.ds(0, LIVE)
    small = [
        pltpu.make_async_copy(src.at[live_rows, :], dst, in_sem.at[i])
        for i, (src, dst) in enumerate(((q_hbm, q), (k_hbm, k), (v_hbm, v), (res_hbm, res)))
    ]
    small.append(pltpu.make_async_copy(wo_hbm, wo, in_sem.at[4]))
    for copy in small:
        copy.start()
    deep = widths(model, 512)
    wide = widths(model, 512)
    gate_in = [
        pltpu.make_async_copy(wg_hbm.at[pl.ds(at, w), :], wg.at[pl.ds(at, w), :], gate_sem.at[i])
        for i, (at, w) in enumerate(deep)
    ]
    up_in = [
        pltpu.make_async_copy(wu_hbm.at[pl.ds(at, w), :], wu.at[pl.ds(at, w), :], up_sem.at[i])
        for i, (at, w) in enumerate(deep)
    ]
    down_in = [
        pltpu.make_async_copy(wd_hbm.at[:, pl.ds(at, w)], wd.at[:, pl.ds(at, w)], down_sem.at[i])
        for i, (at, w) in enumerate(wide)
    ]
    for copy in small[:3]:
        copy.wait()
    for one, two in zip(gate_in, up_in):
        one.start()
        two.start()
    for copy in down_in:
        copy.start()

    row_at = lax.broadcasted_iota(jnp.int32, (LIVE, LIVE), 0)
    col_at = lax.broadcasted_iota(jnp.int32, (LIVE, LIVE), 1)
    row_flow = jnp.zeros((LIVE, LIVE), jnp.int32)
    col_flow = jnp.zeros((LIVE, LIVE), jnp.int32)
    end = jnp.int32(0)
    for flow in range(lens.shape[1]):
        end = end + lens[0, flow]
        row_flow += (row_at >= end).astype(jnp.int32)
        col_flow += (col_at >= end).astype(jnp.int32)
    total_live = end
    same = row_flow == col_flow
    heads = [slice(at, at + HEAD) for at in range(0, width, HEAD)]
    scores = [
        lax.dot_general(
            q[:, cols], k[:, cols], (((1,), (1,)), ((), ())), preferred_element_type=F32
        )
        for cols in heads
    ]
    scores = [jnp.where(same, score * HEAD ** (-0.5), -jnp.inf) for score in scores]
    tops = [jnp.max(score, axis=1, keepdims=True) for score in scores]
    weights = [jnp.exp(score - top) for score, top in zip(scores, tops)]
    sums = [jnp.sum(weight, axis=1, keepdims=True) for weight in weights]
    probs = [(weight / total).astype(BF16) for weight, total in zip(weights, sums)]
    outs = [
        jnp.dot(prob, v[:, cols], preferred_element_type=F32).astype(BF16)
        for prob, cols in zip(probs, heads)
    ]
    for cols, value in zip(heads, outs):
        mixed[:, cols] = value

    small[3].wait()
    small[4].wait()
    pl.semaphore_wait(barrier, n_attn * n_ffn - 1)
    sent = []
    first = {}
    for i, (at, w) in enumerate(wide):
        for sub in range(at, at + w, width):
            cols = slice(sub, sub + width)
            value = jnp.dot(mixed[...], wo[:, cols], preferred_element_type=F32)
            value += jnp.where(a == sub // width, res[...].astype(F32), 0.0)
            term[:, cols] = value
            term16[:, cols] = value.astype(BF16)
        for step in sorted(range(1, n_attn), key=lambda far: -min(far, n_attn - far)):
            peer = lax.rem(a + step, n_attn)
            peer_rows = pl.ds(pl.multiple_of(lax.rem(peer, PARTS) * ROWS, ROWS), ROWS)
            copy = pltpu.make_async_remote_copy(
                src_ref=term16.at[peer_rows, pl.ds(at, w)],
                dst_ref=got1.at[step - 1, :, pl.ds(at, w)],
                send_sem=send1.at[step - 1, i],
                recv_sem=recv1.at[step - 1, i],
                device_id={"attn": peer},
                device_id_type=MESH,
            )
            copy.start()
            sent.append(copy)
            first[i, step] = copy

    second = []
    for i, (at, w) in enumerate(deep):
        cols = slice(at, at + w)
        value = term[own_rows, cols]
        for step in range(1, n_attn):
            first[i, step].wait_recv()
            value += got1[step - 1, :, cols].astype(F32)
        state[:, cols] = value
        rows[0:ROWS, cols] = value.astype(BF16)
        for step in range(1, n_ffn):
            copy = pltpu.make_async_remote_copy(
                src_ref=rows.at[pl.ds(0, ROWS), pl.ds(at, w)],
                dst_ref=rows.at[pl.ds(step * ROWS, ROWS), pl.ds(at, w)],
                send_sem=send2.at[step - 1, i],
                recv_sem=recv2.at[step - 1, i],
                device_id={"ffn": lax.rem(z + step, n_ffn)},
                device_id_type=MESH,
            )
            copy.start()
            sent.append(copy)
            second.append(copy)
    state_copy = pltpu.make_async_remote_copy(
        src_ref=state,
        dst_ref=held.at[place],
        send_sem=send4.at[0],
        recv_sem=recv4.at[place],
        device_id={"attn": owner},
        device_id_type=MESH,
    )

    @pl.when(away)
    def _():
        state_copy.start()

    @pl.when(a == owner)
    def _():
        held[place] = state[...]

    squares = jnp.zeros((n_ffn * ROWS, 1), F32)
    for i, (at, w) in enumerate(deep):
        gate_in[i].wait()
        up_in[i].wait()
        for step in range(1, n_ffn):
            second[i * (n_ffn - 1) + step - 1].wait_recv()
        piece = rows[:, at : at + w]
        squares += jnp.sum(piece.astype(F32) * piece.astype(F32), axis=1, keepdims=True)
        scale = lax.rsqrt(squares / model + 1e-06)
        for col, cw in widths(units, 512):
            cols = slice(col, col + cw)
            g = jnp.dot(piece, wg[at : at + w, cols], preferred_element_type=F32)
            u = jnp.dot(piece, wu[at : at + w, cols], preferred_element_type=F32)
            if i > 0:
                g += gate[:, cols]
                u += up[:, cols]
            if i < len(deep) - 1:
                gate[:, cols] = g
                up[:, cols] = u
            else:
                g *= scale
                u *= scale
                hidden[:, cols] = (g / (1.0 + jnp.exp(-g)) * u).astype(BF16)

    def partial(step, i, at, w):
        return pltpu.make_async_remote_copy(
            src_ref=part16.at[pl.ds(step * ROWS, ROWS), pl.ds(at, w)],
            dst_ref=got2.at[place, step, :, pl.ds(at, w)],
            send_sem=send3.at[step, i],
            recv_sem=recv3.at[place, step, i],
            device_id={"ffn": lax.rem(z + n_ffn - step, n_ffn), "attn": owner},
            device_id_type=MESH,
        )

    for i, (at, w) in enumerate(wide):
        cols = slice(at, at + w)
        down_in[i].wait()
        part16[:, cols] = jnp.dot(hidden[...], wd[:, cols], preferred_element_type=F32).astype(BF16)

        @pl.when(a < PARTS)
        def _():
            for step in range(1, n_ffn):
                partial(step, i, at, w).start()

        @pl.when(away)
        def _():
            partial(0, i, at, w).start()

        @pl.when(a == owner)
        def _():
            got2[place, 0, :, cols] = part16[0:ROWS, cols]

    per = share // ROWS

    @pl.when(a * share >= LIVE)
    def _():
        out[...] = jnp.zeros_like(out)

    @pl.when(a * share < LIVE)
    def _():
        def arrival(q, step, i, at, w):
            return pltpu.make_async_remote_copy(
                src_ref=part16.at[pl.ds(step * ROWS, ROWS), pl.ds(at, w)],
                dst_ref=got2.at[q, step, :, pl.ds(at, w)],
                send_sem=send3.at[step, i],
                recv_sem=recv3.at[q, step, i],
                device_id={"attn": owner},
                device_id_type=MESH,
            )

        for q in range(per):

            @pl.when(a * per + q != a)
            def _():
                pltpu.make_async_remote_copy(
                    src_ref=state,
                    dst_ref=held.at[q],
                    send_sem=send4.at[0],
                    recv_sem=recv4.at[q],
                    device_id={"attn": owner},
                    device_id_type=MESH,
                ).wait_recv()

        at_row = lax.broadcasted_iota(jnp.int32, (ROWS, 1), 0)
        for i, (at, w) in enumerate(wide):
            cols = slice(at, at + w)
            for q in range(per):

                @pl.when(a * per + q != a)
                def _():
                    arrival(q, 0, i, at, w).wait_recv()

                for step in range(1, n_ffn):
                    arrival(q, step, i, at, w).wait_recv()
                feed = got2[q, 0, :, cols].astype(F32)
                for step in range(1, n_ffn):
                    feed += got2[q, step, :, cols].astype(F32)
                live = (a * per + q) * ROWS + at_row < total_live
                value = jnp.where(live, held[q, :, cols] + feed, 0.0)
                out[q * ROWS : (q + 1) * ROWS, cols] = value.astype(BF16)

    for copy in sent:
        copy.wait_send()

    @pl.when(a < PARTS)
    def _():
        for i, (at, w) in enumerate(wide):
            for step in range(1, n_ffn):
                partial(step, i, at, w).wait_send()

    @pl.when(away)
    def _():
        state_copy.wait_send()
        for i, (at, w) in enumerate(wide):
            partial(0, i, at, w).wait_send()


def on_device(n_attn, n_ffn, q, k, v, res, lens, wo, wg, wu, wd):
    group, width = q.shape
    model = wo.shape[1]
    units = wg.shape[1]
    share = group // n_attn
    tokens = n_ffn * ROWS
    per = share // ROWS
    pieces = max(1, model // 512)
    any_space = pl.BlockSpec(memory_space=pl.ANY)
    dma = pltpu.SemaphoreType.DMA
    return pl.pallas_call(
        functools.partial(layer, n_attn, n_ffn),
        out_shape=pltpu.VMEM((share, model), BF16),
        in_specs=[any_space] * 4 + [pl.BlockSpec(memory_space=pltpu.SMEM)] + [any_space] * 4,
        out_specs=pl.BlockSpec(memory_space=pltpu.VMEM),
        scratch_shapes=[
            pltpu.VMEM((LIVE, width), BF16),
            pltpu.VMEM((LIVE, width), BF16),
            pltpu.VMEM((LIVE, width), BF16),
            pltpu.VMEM((LIVE, width), BF16),
            pltpu.VMEM((width, model), BF16),
            pltpu.VMEM((model, units), BF16),
            pltpu.VMEM((model, units), BF16),
            pltpu.VMEM((units, model), BF16),
            pltpu.VMEM((LIVE, width), BF16),
            pltpu.VMEM((LIVE, model), F32),
            pltpu.VMEM((LIVE, model), BF16),
            pltpu.VMEM((n_attn - 1, ROWS, model), BF16),
            pltpu.VMEM((ROWS, model), F32),
            pltpu.VMEM((tokens, model), BF16),
            pltpu.VMEM((tokens, units), F32),
            pltpu.VMEM((tokens, units), F32),
            pltpu.VMEM((tokens, units), BF16),
            pltpu.VMEM((tokens, model), BF16),
            pltpu.VMEM((per, n_ffn, ROWS, model), BF16),
            pltpu.VMEM((per, ROWS, model), F32),
            dma((5,)),
            dma((pieces,)),
            dma((pieces,)),
            dma((pieces,)),
            dma((n_attn - 1, pieces)),
            dma((n_attn - 1, pieces)),
            dma((n_ffn - 1, pieces)),
            dma((n_ffn - 1, pieces)),
            dma((n_ffn, pieces)),
            dma((per, n_ffn, pieces)),
            dma((1,)),
            dma((per,)),
        ],
        compiler_params=pltpu.CompilerParams(
            collective_id=0, has_side_effects=True, vmem_limit_bytes=56 * 1024 * 1024
        ),
        cost_estimate=pl.CostEstimate(
            flops=2 * tokens * 3 * model * units + 2 * LIVE * width * model,
            bytes_accessed=2 * (3 * model * units + width * model),
            transcendentals=tokens * units,
        ),
    )(q, k, v, res, lens, wo, wg, wu, wd)


def solution(mesh):
    rows_split = P(("dom", "ffn"), "attn")
    placed = (
        rows_split,
        rows_split,
        rows_split,
        rows_split,
        P(("dom", "ffn"), None),
        P("attn", None),
        P(None, "ffn"),
        P(None, "ffn"),
        P("ffn", None),
    )
    return jax.shard_map(
        functools.partial(on_device, mesh.shape["attn"], mesh.shape["ffn"]),
        mesh=mesh,
        in_specs=placed,
        out_specs=P(("dom", "ffn", "attn"), None),
        check_vma=False,
    )
```
